1024 devices in a mesh: loop: 128 (over z, y_lo, core), rep: 8 (over x, y_hi).
Axes of the slice: x: 4, y: 8 (y_hi: 2, y_lo: 4; y = y_hi * 4 + y_lo), z: 16, core: 2. Of those that a mesh axis runs over, the one named last changes fastest.
Arguments:
- features: bfloat16 [512, 16384], P('rep', 'loop'), may hold values from -6 to 6
- cotangent: bfloat16 [512, 16384], P('rep', 'loop'), may hold values from -6 to 6
- w_self: bfloat16 [512, 512], replicated, may hold values from -0.25 to 0.25
- w_neigh: bfloat16 [512, 512], replicated, may hold values from -0.25 to 0.25
- tile_cols: int32 [128, 16], P('loop'), may hold values from 0 to 127, as said below
- tile_edges: int32 [128, 16, 128, 128], P('loop'), may hold values from 0 to 3, as said below
- degrees: int32 [16384], P('loop'), may hold values from 0 to 6144, as said below
Outputs:
- layer_out: bfloat16 [512, 16384], P('rep', 'loop')
- input_grad: bfloat16 [512, 16384], P('rep', 'loop')
- grad_self: float32 [512, 512], P('rep')
- grad_neigh: float32 [512, 512], P('rep')
The draws below stay inside these ranges and needn't reach their ends.
Inputs may be any that keep to these rules, and one draw needn't show every extreme that they name: `tile_cols`: slot 0 of block row b names b itself; every block row has 1 to 16 live slots in front, their number varying strongly from row to row, and exactly 16 in some block row; the remaining slots name any block and hold zero tiles. In that full block row one node has 3 edges to every column node of every slot. `tile_edges`: edge counts of the tiles; zero in slots after a row's live ones; some nodes have no edges at all. `degrees`: each node's degree equals the sum of its row of A; exactly one node reaches the most.
All inputs are finite; a program needn't handle non-finite values.
Results may differ from the reference program's by a relative error of at most 0.008.
Values may be sent and summed in bfloat16 or wider, within the bound.
No kernel may reach another device: no remote copies, remote signals or barrier semaphores. Data moves between devices by JAX's collectives and lax.ppermute only.
A program may use at most 32 MiB of HBM per device.

```python
import math
import jax
import jax.numpy as jnp
from jax import lax

D = 512
TILE = 128
SLOTS = 16
BLOCKS = 128
NODES = 16384


def pattern(key):
    keys = jax.random.split(key, 7)
    first_draw = jax.random.randint(keys[0], (BLOCKS,), 0, SLOTS)
    second_draw = jax.random.randint(keys[1], (BLOCKS,), 1, SLOTS + 1)
    live_count = jnp.minimum(SLOTS, 1 + 2 * first_draw * second_draw // SLOTS)
    full_row = jax.random.randint(keys[2], (), 0, BLOCKS)
    block_ids = jnp.arange(BLOCKS, dtype=jnp.int32)
    live_count = jnp.where(block_ids == full_row, SLOTS, live_count)
    slot_ids = jnp.arange(SLOTS, dtype=jnp.int32)
    column_ids = jax.random.randint(keys[3], (BLOCKS, SLOTS), 0, BLOCKS)
    column_ids = jnp.where(slot_ids[None, :] == 0, block_ids[:, None], column_ids)
    raw_draw = jax.random.randint(keys[4], (BLOCKS, SLOTS, TILE, TILE), 0, 256)
    edge_counts = jnp.where(raw_draw >= 253, raw_draw - 252, 0)
    live_mask = (slot_ids[None, :] < live_count[:, None]).astype(jnp.int32)
    kept_rows = (jax.random.randint(keys[5], (BLOCKS, 1, TILE, 1), 0, 16) != 0).astype(jnp.int32)
    edge_counts = edge_counts * live_mask[:, :, None, None] * kept_rows
    full_node = jax.random.randint(keys[6], (), 0, TILE)
    node_ids = jnp.arange(TILE, dtype=jnp.int32)
    dense_row = (block_ids[:, None, None, None] == full_row) & (node_ids[None, None, :, None] == full_node)
    edge_counts = jnp.where(dense_row, 3, edge_counts)
    return (column_ids.astype(jnp.int32), edge_counts.astype(jnp.int32))


def draw_tile_cols(key, part):
    return pattern(key)[0]


def draw_tile_edges(key, part):
    return pattern(key)[1]


def draw_degrees(key, part):
    edge_counts = pattern(key)[1]
    return jnp.sum(edge_counts, axis=(1, 3)).reshape(NODES).astype(jnp.int32)


def steps_of(stream_key, extent, cuts, smallest, high):
    factor_of, own = 1.0, jax.random.fold_in(stream_key, 6)
    for axis_at, blocks in cuts:
        heights = jnp.exp(jax.random.uniform(jax.random.fold_in(own, axis_at), (blocks,), jnp.float32, smallest / len(cuts), high / len(cuts)))
        factor_of = factor_of * jnp.repeat(heights, extent[axis_at] // blocks).reshape([-1 if axis == axis_at else 1 for axis in range(len(extent))])
    return factor_of


def normal_values(stream_key, shape, scale, most, cuts=(), kind=jnp.bfloat16):
    array = jax.random.normal(stream_key, shape, jnp.float32) * scale
    if len(cuts) > 0:
        array = steps_of(stream_key, shape, cuts, -0.22, 0.18) * array
    return jnp.clip(array, min=-most, max=most).astype(kind)


def setup_inputs(seed: int = 0) -> dict:
    seeds = jax.random.split(jax.random.key(seed), 8)
    features = normal_values(seeds[0], (D, NODES), 1.0, 6.0, ((0, 8), (1, 128)))
    cotangent = normal_values(seeds[1], (D, NODES), 1.0, 6.0, ((0, 8), (1, 128)))
    w_self = normal_values(seeds[2], (D, D), D ** -0.5, 0.25)
    w_neigh = normal_values(seeds[3], (D, D), D ** -0.5, 0.25)
    tile_cols = draw_tile_cols(jax.random.fold_in(seeds[7], 71), 0)
    tile_edges = draw_tile_edges(jax.random.fold_in(seeds[7], 71), 0)
    degrees = draw_degrees(jax.random.fold_in(seeds[7], 71), 0)
    return dict(features=features, cotangent=cotangent, w_self=w_self, w_neigh=w_neigh, tile_cols=tile_cols, tile_edges=tile_edges, degrees=degrees)


def reference(features, cotangent, w_self, w_neigh, tile_cols, tile_edges, degrees):
    edge_values = tile_edges.astype(jnp.float32)
    divisor = jnp.maximum(degrees.astype(jnp.float32), 1.0).reshape(BLOCKS, TILE)
    blocks = features.reshape(D, BLOCKS, TILE)
    chosen = jnp.take(blocks, tile_cols.reshape(-1), axis=1).reshape(D, BLOCKS, SLOTS, TILE)
    totals = jnp.einsum('dbkc,bkrc->dbr', chosen.astype(jnp.float32), edge_values)
    neighbours = (totals / divisor).astype(jnp.bfloat16).reshape(D, NODES)
    forward = jnp.dot(w_self.T, features, preferred_element_type=jnp.float32) + jnp.dot(w_neigh.T, neighbours, preferred_element_type=jnp.float32)
    layer_out = forward.astype(jnp.bfloat16)
    scaled = cotangent.astype(jnp.float32).reshape(D, BLOCKS, TILE) / divisor
    spread = jnp.einsum('obr,bkrc->bkoc', scaled, edge_values, precision=lax.Precision.HIGHEST)
    onehot = (tile_cols[:, :, None] == jnp.arange(BLOCKS, dtype=jnp.int32)[None, None, :]).astype(jnp.float32)
    pulled = jnp.einsum('bkj,bkoc->joc', onehot, spread, precision=lax.Precision.HIGHEST)
    pulled_rows = pulled.transpose(1, 0, 2).reshape(D, NODES).astype(jnp.bfloat16)
    backward = jnp.dot(w_self, cotangent, preferred_element_type=jnp.float32) + jnp.dot(w_neigh, pulled_rows, preferred_element_type=jnp.float32)
    input_grad = backward.astype(jnp.bfloat16)
    factor = 1.0 / math.sqrt(NODES)
    grad_self = jnp.dot(features, cotangent.T, preferred_element_type=jnp.float32) * factor
    grad_neigh = jnp.dot(neighbours, cotangent.T, preferred_element_type=jnp.float32) * factor
    return (layer_out, input_grad, grad_self, grad_neigh)
```

```python
import math

import jax
import jax.numpy as jnp
from jax import lax
from jax.experimental import pallas as pl
from jax.experimental.pallas import tpu as pltpu
from jax.sharding import Mesh, PartitionSpec as P

F32, BF16 = jnp.float32, jnp.bfloat16
LOOP = (16, 4, 2)


def place(col):
    depth, rows, cores = LOOP
    row = lax.rem(lax.div(col, cores), rows)
    return lax.rem(col, cores), row * depth + lax.div(col, cores * rows)


def contribute(cols, rep, cot_all, degrees, tiles, w_self, w_neigh, out, own_term, held):
    slots, rows = tiles.shape[1], out.shape[1]

    def clear(i, _):
        out[i] = jnp.zeros(out.shape[1:], out.dtype)
        return 0

    lax.fori_loop(0, out.shape[0], clear, 0)
    own = pl.ds(pl.multiple_of(rep[0] * rows, rows), rows)
    cot = cot_all[...].reshape(w_self.shape[0], out.shape[2])
    own_term[...] = jnp.dot(w_self[own, :], cot, preferred_element_type=F32)
    scaled = jnp.dot(w_neigh[own, :], cot, preferred_element_type=F32)
    scaled = scaled / jnp.maximum(degrees[...].astype(F32), 1.0)
    high = scaled.astype(BF16)
    low = (scaled - high.astype(F32)).astype(BF16)
    both = jnp.concatenate([high, low], 0)
    for k in range(slots):
        part = jnp.dot(both, tiles[0, k].astype(F32).astype(BF16), preferred_element_type=F32)
        held[k] = part[:rows] + part[rows:]
    first = []
    for k in range(slots):
        at = jnp.int32(k)
        for j in range(k - 1, -1, -1):
            at = jnp.where(cols[0, j] == cols[0, k], jnp.int32(j), at)
        first.append(at)
    for k in range(1, slots):

        @pl.when(first[k] != k)
        def _():
            held[first[k]] = held[first[k]] + held[k]

    for k in range(slots):

        @pl.when(first[k] == k)
        def _():
            core, at = place(cols[0, k])
            out[core * (out.shape[0] // LOOP[2]) + at] = held[k].astype(out.dtype)


def combine(cols, here, features, cot_all, degrees, tiles, near, far, w_self, w_neigh, out, grads):
    slots, rows = tiles.shape[1], features.shape[0]
    total = jnp.zeros(features.shape, F32)
    for k in range(slots):
        core, at = place(cols[0, k])
        total = total + lax.dot_general(
            jnp.where(core == here[1], near[at], far[at]),
            tiles[0, k].astype(F32).astype(BF16),
            (((1,), (1,)), ((), ())),
            preferred_element_type=F32,
        )
    mean = (total / jnp.maximum(degrees[...].astype(F32), 1.0)).astype(BF16)
    own = pl.ds(pl.multiple_of(here[0] * rows, rows), rows)
    flip = (((0,), (0,)), ((), ()))
    forward = lax.dot_general(w_self[own, :], features[...], flip, preferred_element_type=F32)
    forward = forward + lax.dot_general(w_neigh[own, :], mean, flip, preferred_element_type=F32)
    both = jnp.concatenate([features[...], mean], 0)
    for r in range(out.shape[0]):
        out[r] = forward[r * rows : (r + 1) * rows].astype(BF16)
        term = lax.dot_general(both, cot_all[r], (((1,), (1,)), ((), ())), preferred_element_type=F32)
        grads[0, :, r * rows : (r + 1) * rows] = term[:rows]
        grads[1, :, r * rows : (r + 1) * rows] = term[rows:]


VMEM = pl.BlockSpec(memory_space=pltpu.VMEM)
SMEM = pl.BlockSpec(memory_space=pltpu.SMEM)
PARAMS = pltpu.CompilerParams(vmem_limit_bytes=32 * 1024 * 1024)


def body(features, cotangent, w_self, w_neigh, tile_cols, tile_edges, degrees):
    depth, ring, cores = LOOP
    rows, size = features.shape
    total = w_self.shape[0]
    reps = total // rows
    blocks = depth * ring * cores
    degrees = degrees.reshape(1, size)
    rep = lax.axis_index("rep").astype(jnp.int32)
    here = jnp.stack([rep, lax.axis_index("c").astype(jnp.int32)])

    def spread(array, axis, parts):
        return lax.all_to_all(jnp.broadcast_to(array[None], (parts, *array.shape)), axis, 0, 0)

    def fold(array, axis, parts):
        given = lax.all_to_all(array.reshape(parts, -1, *array.shape[1:]), axis, 0, 0)
        return jnp.sum(given.astype(F32), 0)

    panels = spread(features, "z", depth)
    cot_all = spread(cotangent, "rep", reps)
    near = spread(panels, "y", ring).reshape(blocks // cores, rows, size)
    far = lax.ppermute(near, "c", [(0, 1), (1, 0)])
    shares, own_term = pl.pallas_call(
        contribute,
        out_shape=(
            jax.ShapeDtypeStruct((blocks, rows, size), BF16),
            jax.ShapeDtypeStruct((rows, size), F32),
        ),
        in_specs=[SMEM, SMEM] + [VMEM] * 5,
        out_specs=(VMEM, VMEM),
        scratch_shapes=[pltpu.VMEM((tile_edges.shape[1], rows, size), F32)],
        compiler_params=PARAMS,
        name="contribute",
    )(tile_cols, here, cot_all, degrees, tile_edges, w_self, w_neigh)
    shares = fold(shares, "c", cores).astype(BF16)
    shares = fold(shares, "y", ring).astype(BF16)
    pulled = fold(shares, "z", depth)[0]
    input_grad = (own_term + pulled).astype(BF16)

    terms, grads = pl.pallas_call(
        combine,
        out_shape=(
            jax.ShapeDtypeStruct((reps, rows, size), BF16),
            jax.ShapeDtypeStruct((2, rows, total), F32),
        ),
        in_specs=[SMEM, SMEM] + [VMEM] * 8,
        out_specs=(VMEM, VMEM),
        compiler_params=PARAMS,
        name="combine",
    )(tile_cols, here, features, cot_all, degrees, tile_edges, near, far, w_self, w_neigh)
    layer_out = fold(terms, "rep", reps)[0].astype(BF16)
    grads = fold(grads, "c", cores)[0]
    grads = fold(grads, "y", ring).astype(BF16)
    grads = spread(grads, "z", depth).astype(F32).sum(0) * (1.0 / math.sqrt(blocks * size))
    grads = spread(grads, "y", ring).reshape(rows, total)
    grads = spread(grads, "c", cores)
    return layer_out, input_grad, grads[0], grads[1]


def solution(mesh):
    fine = Mesh(mesh.devices.reshape(*LOOP, mesh.shape["rep"]), ("z", "y", "c", "rep"))
    loop = ("z", "y", "c")
    in_specs = (
        P("rep", loop),
        P("rep", loop),
        P(),
        P(),
        P(loop, None),
        P(loop, None, None, None),
        P(loop),
    )
    out_specs = (P("rep", loop), P("rep", loop), P("rep", None), P("rep", None))
    return jax.shard_map(body, mesh=fine, in_specs=in_specs, out_specs=out_specs, check_vma=False)
```

```python
import functools
import math

import jax
import jax.numpy as jnp
from jax import lax
from jax.experimental import pallas as pl
from jax.experimental.pallas import tpu as pltpu
from jax.sharding import Mesh, PartitionSpec as P

F32, BF16 = jnp.float32, jnp.bfloat16
AXES = ("zh", "zm", "zl", "yh", "yl", "c")
LOOP = (4, 2, 2, 2, 2, 2)
NEAR, MID, FAR = ("zl", "yl"), ("zm", "yh"), ("zh",)


def count(axes):
    return math.prod(LOOP[AXES.index(axis)] for axis in axes)


def place(col):
    digit = {}
    for axis, extent in zip(reversed(AXES), reversed(LOOP)):
        digit[axis] = lax.rem(col, extent)
        col = lax.div(col, extent)
    near = far = jnp.int32(0)
    for axis in NEAR:
        near = near * LOOP[AXES.index(axis)] + digit[axis]
    for axis in MID + FAR:
        far = far * LOOP[AXES.index(axis)] + digit[axis]
    return digit["c"], near, far


def split(value):
    high = value.astype(BF16)
    return jnp.concatenate([high, (value - high.astype(F32)).astype(BF16)], 0)


def join(pair):
    half = pair.shape[0] // 2
    return pair[:half].astype(F32) + pair[half:].astype(F32)


def combine(cols, here, features, cot, degrees, tiles, near, far, w_self, w_neigh, out, neighbours):
    slots, rows = tiles.shape[1], features.shape[0]
    total = jnp.zeros(features.shape, F32)
    for k in range(slots):
        core, i, j = place(cols[0, k])
        at = i * count(MID + FAR) + j
        total = total + lax.dot_general(
            jnp.where(core == here[1], near[at], far[at]),
            tiles[0, k].astype(F32).astype(BF16),
            (((1,), (1,)), ((), ())),
            preferred_element_type=F32,
        )
    mean = (total / jnp.maximum(degrees[...].astype(F32), 1.0)).astype(BF16)
    neighbours[...] = mean
    own = pl.ds(pl.multiple_of(here[0] * rows, rows), rows)
    flip = (((0,), (0,)), ((), ()))
    forward = lax.dot_general(w_self[own, :], features[...], flip, preferred_element_type=F32)
    forward = forward + lax.dot_general(w_neigh[own, :], mean, flip, preferred_element_type=F32)
    for r in range(out.shape[0]):
        out[r, 0] = forward[r * rows : (r + 1) * rows].astype(BF16)
        out[r, 1] = cot[...]


def contribute(
    cols, here, parts, features, neighbours, degrees, tiles, w_self, w_neigh, layer_out, own_term, mine, theirs, held
):
    slots, rows, size = tiles.shape[1], features.shape[0], w_self.shape[0]
    members, filled = mine.shape[0], count(MID + FAR) * rows
    empty = jnp.zeros((rows, mine.shape[2]), BF16)

    def clear(i, _):
        for j in range(0, filled, rows):
            mine[i, j : j + rows] = empty
            theirs[i, j : j + rows] = empty
        return 0

    lax.fori_loop(0, members, clear, 0)
    forward = parts[0, 0].astype(F32)
    for r in range(1, parts.shape[0]):
        forward = forward + parts[r, 0].astype(F32)
    layer_out[...] = forward.astype(BF16)
    cot = parts[:, 1].reshape(size, parts.shape[3])
    own = pl.ds(pl.multiple_of(here[0] * rows, rows), rows)
    own_term[...] = jnp.dot(w_self[own, :], cot, preferred_element_type=F32)
    scaled = jnp.dot(w_neigh[own, :], cot, preferred_element_type=F32)
    both = split(scaled / jnp.maximum(degrees[...].astype(F32), 1.0))
    for k in range(slots):
        part = jnp.dot(both, tiles[0, k].astype(F32).astype(BF16), preferred_element_type=F32)
        held[k] = part[:rows] + part[rows:]
    first = []
    for k in range(slots):
        at = jnp.int32(k)
        for j in range(k - 1, -1, -1):
            at = jnp.where(cols[0, j] == cols[0, k], jnp.int32(j), at)
        first.append(at)
    for k in range(1, slots):

        @pl.when(first[k] != k)
        def _():
            held[first[k]] = held[first[k]] + held[k]

    for k in range(slots):
        core, i, j = place(cols[0, k])
        span = pl.ds(pl.multiple_of(j * rows, rows), rows)

        @pl.when((first[k] == k) & (core == here[1]))
        def _():
            mine[i, span, :] = held[k].astype(BF16)

        @pl.when((first[k] == k) & (core != here[1]))
        def _():
            theirs[i, span, :] = held[k].astype(BF16)

    wide = mine.shape[2]
    lanes = size // wide
    high = rows * lanes // members
    pair = jnp.concatenate([features[...], neighbours[...]], 0)
    for q in range(lanes):
        term = lax.dot_general(
            pair, cot[q * wide : (q + 1) * wide], (((1,), (1,)), ((), ())), preferred_element_type=F32
        )
        ours = jnp.where(here[1] == 0, term[:rows], term[rows:])
        other = jnp.where(here[1] == 0, term[rows:], term[:rows])
        for g in range(members // lanes):
            mine[g * lanes + q, filled:] = split(ours[g * high : (g + 1) * high])
            theirs[g * lanes + q, filled:] = split(other[g * high : (g + 1) * high])


def pair_sum(mine, given, out, *, rows):
    filled = count(MID + FAR) * rows

    def step(i, _):
        for j in range(0, filled, rows):
            block = mine[i, j : j + rows].astype(F32) + given[i, j : j + rows].astype(F32)
            out[i, j : j + rows] = block.astype(BF16)
        out[i, filled:] = split(join(mine[i, filled:]) + join(given[i, filled:]))
        return 0

    lax.fori_loop(0, out.shape[0], step, 0)


def stage_sum(given, out, *, rows, cut):
    members = out.shape[0]
    blocks = count(FAR) if cut else 1
    for j in range(members):
        for k in range(blocks):
            at = (j * blocks + k) * rows
            total = given[0, at : at + rows].astype(F32)
            for i in range(1, given.shape[0]):
                total = total + given[i, at : at + rows].astype(F32)
            out[j, k * rows : (k + 1) * rows] = total.astype(BF16)
    start = members * blocks * rows
    piece = join(given[0, start:])
    for i in range(1, given.shape[0]):
        piece = piece + join(given[i, start:])
    high = piece.shape[0] // members
    for j in range(members):
        out[j, blocks * rows :] = split(piece[j * high : (j + 1) * high] if cut else piece)


def far_sum(given, own_term, input_grad, pieces, *, factor):
    rows = own_term.shape[0]
    total = own_term[...]
    piece = join(given[0, rows:])
    for j in range(given.shape[0]):
        total = total + given[j, :rows].astype(F32)
        if j > 0:
            piece = piece + join(given[j, rows:])
    input_grad[...] = total.astype(BF16)
    for i in range(pieces.shape[0]):
        pieces[i] = piece * factor


def lay(given, grad_self, grad_neigh):
    _, high, wide = given.shape
    lanes, cuts = grad_self.shape[1] // wide, count(MID)
    half = given.shape[0] // 2
    for i in range(half):
        piece, part = divmod(i, cuts)
        g, q = divmod(piece, lanes)
        top = (g * cuts + part) * high
        grad_self[top : top + high, q * wide : (q + 1) * wide] = given[i]
        grad_neigh[top : top + high, q * wide : (q + 1) * wide] = given[half + i]


def run(kernel, outs, scalars, arrays, scratch=(), name=None):
    vmem = pl.BlockSpec(memory_space=pltpu.VMEM)
    smem = pl.BlockSpec(memory_space=pltpu.SMEM)
    return pl.pallas_call(
        kernel,
        out_shape=tuple(jax.ShapeDtypeStruct(shape, kind) for shape, kind in outs),
        in_specs=[smem] * len(scalars) + [vmem] * len(arrays),
        out_specs=(vmem,) * len(outs),
        scratch_shapes=[pltpu.VMEM(shape, kind) for shape, kind in scratch],
        compiler_params=pltpu.CompilerParams(vmem_limit_bytes=32 * 1024 * 1024),
        name=name,
    )(*scalars, *arrays)


def spread(array, axes):
    parts = count(axes)
    return lax.all_to_all(jnp.broadcast_to(array[None], (parts, *array.shape)), axes, 0, 0)


def body(features, cotangent, w_self, w_neigh, tile_cols, tile_edges, degrees):
    rows, size = features.shape
    total = w_self.shape[0]
    reps = total // rows
    blocks, near_count, mid_count, far_count = math.prod(LOOP), count(NEAR), count(MID), count(FAR)
    degrees = degrees.reshape(1, size)
    here = jnp.stack([lax.axis_index("rep").astype(jnp.int32), lax.axis_index("c").astype(jnp.int32)])
    swap = [(0, 1), (1, 0)]
    panel = (rows, size)

    near = spread(spread(features, MID + FAR), NEAR).reshape(blocks // 2, rows, size)
    far = lax.ppermute(near, "c", swap)
    sent, neighbours = run(
        combine,
        [((reps, 2, rows, size), BF16), (panel, BF16)],
        [tile_cols, here],
        [features, cotangent, degrees, tile_edges, near, far, w_self, w_neigh],
        name="combine",
    )
    parts = lax.all_to_all(sent, "rep", 0, 0)

    pieces = 2 * rows * (total // size) // near_count
    stage = ((near_count, mid_count * far_count * rows + pieces, size), BF16)
    layer_out, own_term, mine, theirs = run(
        contribute,
        [(panel, BF16), (panel, F32), stage, stage],
        [tile_cols, here],
        [parts, features, neighbours, degrees, tile_edges, w_self, w_neigh],
        [((tile_edges.shape[1], rows, size), F32)],
        name="contribute",
    )
    given = lax.ppermute(theirs, "c", swap)
    (sums,) = run(functools.partial(pair_sum, rows=rows), [stage], [], [mine, given], name="pair_sum")
    given = lax.all_to_all(sums, NEAR, 0, 0)
    pieces = pieces // mid_count
    (sums,) = run(
        functools.partial(stage_sum, rows=rows, cut=True),
        [((mid_count, far_count * rows + pieces, size), BF16)],
        [],
        [given],
        name="near_sum",
    )
    given = lax.all_to_all(sums, MID, 0, 0)
    (sums,) = run(
        functools.partial(stage_sum, rows=rows, cut=False),
        [((far_count, rows + pieces, size), BF16)],
        [],
        [given],
        name="mid_sum",
    )
    given = lax.all_to_all(sums, FAR, 0, 0)

    input_grad, out = run(
        functools.partial(far_sum, factor=1.0 / math.sqrt(blocks * size)),
        [(panel, BF16), ((2 * near_count * mid_count, pieces // 2, size), F32)],
        [],
        [given, own_term],
        name="far_sum",
    )
    given = lax.all_to_all(out, ("c", *NEAR, *MID), 0, 0)
    grad = ((rows, total), F32)
    grad_self, grad_neigh = run(lay, [grad, grad], [], [given], name="lay")
    return layer_out, input_grad, grad_self, grad_neigh


def solution(mesh):
    fine = Mesh(mesh.devices.reshape(*LOOP, mesh.shape["rep"]), (*AXES, "rep"))
    in_specs = (
        P("rep", AXES),
        P("rep", AXES),
        P(),
        P(),
        P(AXES, None),
        P(AXES, None, None, None),
        P(AXES),
    )
    out_specs = (P("rep", AXES), P("rep", AXES), P("rep", None), P("rep", None))
    return jax.shard_map(body, mesh=fine, in_specs=in_specs, out_specs=out_specs, check_vma=False)
```

```python
import functools
import math

import jax
import jax.numpy as jnp
from jax import lax
from jax.experimental import pallas as pl
from jax.experimental.pallas import tpu as pltpu
from jax.sharding import Mesh, PartitionSpec as P

F32, BF16 = jnp.float32, jnp.bfloat16
AXES = ("zh", "zm", "zl", "yh", "yl", "c")
LOOP = (4, 2, 2, 2, 2, 2)
NEAR, MID, FAR = ("yl", "zl"), ("zm", "yh"), ("zh",)


def count(axes):
    return math.prod(LOOP[AXES.index(axis)] for axis in axes)


def place(col):
    digit = {}
    for axis, extent in zip(reversed(AXES), reversed(LOOP)):
        digit[axis] = lax.rem(col, extent)
        col = lax.div(col, extent)
    near = far = jnp.int32(0)
    for axis in NEAR:
        near = near * LOOP[AXES.index(axis)] + digit[axis]
    for axis in MID + FAR:
        far = far * LOOP[AXES.index(axis)] + digit[axis]
    return digit["c"], near, far


def split(value):
    high = value.astype(BF16)
    return jnp.concatenate([high, (value - high.astype(F32)).astype(BF16)], 0)


def join(pair):
    half = pair.shape[0] // 2
    return pair[:half].astype(F32) + pair[half:].astype(F32)


def combine(cols, here, features, cot, degrees, tiles, near, far, w_self, w_neigh, out, neighbours):
    slots, rows = tiles.shape[1], features.shape[0]
    total = jnp.zeros(features.shape, F32)
    for k in range(slots):
        core, i, j = place(cols[0, k])
        at = i * count(MID + FAR) + j
        total = total + lax.dot_general(
            jnp.where(core == here[1], near[at], far[at]),
            tiles[0, k].astype(F32).astype(BF16),
            (((1,), (1,)), ((), ())),
            preferred_element_type=F32,
        )
    mean = (total / jnp.maximum(degrees[...].astype(F32), 1.0)).astype(BF16)
    neighbours[...] = mean
    own = pl.ds(pl.multiple_of(here[0] * rows, rows), rows)
    flip = (((0,), (0,)), ((), ()))
    forward = lax.dot_general(w_self[own, :], features[...], flip, preferred_element_type=F32)
    forward = forward + lax.dot_general(w_neigh[own, :], mean, flip, preferred_element_type=F32)
    for r in range(out.shape[0]):
        out[r, 0] = forward[r * rows : (r + 1) * rows].astype(BF16)
        out[r, 1] = cot[...]


def contribute(
    cols, here, parts, features, neighbours, degrees, tiles, w_self, w_neigh, layer_out, own_term, mine, theirs, held
):
    slots, rows, size = tiles.shape[1], features.shape[0], w_self.shape[0]
    members, filled = mine.shape[0], count(MID + FAR) * rows
    empty = jnp.zeros((rows, mine.shape[2]), BF16)

    def clear(i, _):
        for j in range(0, filled, rows):
            mine[i, j : j + rows] = empty
            theirs[i, j : j + rows] = empty
        return 0

    lax.fori_loop(0, members, clear, 0)
    forward = parts[0, 0].astype(F32)
    for r in range(1, parts.shape[0]):
        forward = forward + parts[r, 0].astype(F32)
    layer_out[...] = forward.astype(BF16)
    cot = parts[:, 1].reshape(size, parts.shape[3])
    own = pl.ds(pl.multiple_of(here[0] * rows, rows), rows)
    own_term[...] = jnp.dot(w_self[own, :], cot, preferred_element_type=F32)
    scaled = jnp.dot(w_neigh[own, :], cot, preferred_element_type=F32)
    both = split(scaled / jnp.maximum(degrees[...].astype(F32), 1.0))
    for k in range(slots):
        part = jnp.dot(both, tiles[0, k].astype(F32).astype(BF16), preferred_element_type=F32)
        held[k] = part[:rows] + part[rows:]
    first = []
    for k in range(slots):
        at = jnp.int32(k)
        for j in range(k - 1, -1, -1):
            at = jnp.where(cols[0, j] == cols[0, k], jnp.int32(j), at)
        first.append(at)
    for k in range(1, slots):

        @pl.when(first[k] != k)
        def _():
            held[first[k]] = held[first[k]] + held[k]

    for k in range(slots):
        core, i, j = place(cols[0, k])
        span = pl.ds(pl.multiple_of(j * rows, rows), rows)

        @pl.when((first[k] == k) & (core == here[1]))
        def _():
            mine[i, span, :] = held[k].astype(BF16)

        @pl.when((first[k] == k) & (core != here[1]))
        def _():
            theirs[i, span, :] = held[k].astype(BF16)

    wide = mine.shape[2]
    lanes = size // wide
    high = rows * lanes // members
    pair = jnp.concatenate([features[...], neighbours[...]], 0)
    for q in range(lanes):
        term = lax.dot_general(
            pair, cot[q * wide : (q + 1) * wide], (((1,), (1,)), ((), ())), preferred_element_type=F32
        )
        ours = jnp.where(here[1] == 0, term[:rows], term[rows:])
        other = jnp.where(here[1] == 0, term[rows:], term[:rows])
        for g in range(members // lanes):
            mine[g * lanes + q, filled:] = split(ours[g * high : (g + 1) * high])
            theirs[g * lanes + q, filled:] = split(other[g * high : (g + 1) * high])


def pair_sum(mine, given, out, *, rows):
    filled = count(MID + FAR) * rows

    def step(i, _):
        for j in range(0, filled, rows):
            block = mine[i, j : j + rows].astype(F32) + given[i, j : j + rows].astype(F32)
            out[i, j : j + rows] = block.astype(BF16)
        out[i, filled:] = (join(mine[i, filled:]) + join(given[i, filled:])).astype(BF16)
        return 0

    lax.fori_loop(0, out.shape[0], step, 0)


def stage_sum(given, out, *, rows):
    members = out.shape[0]
    blocks = (given.shape[1] - out.shape[1]) // ((members - 1) * rows) if members > 1 else 1
    for j in range(members):
        for k in range(blocks):
            at = (j * blocks + k) * rows
            total = given[0, at : at + rows].astype(F32)
            for i in range(1, given.shape[0]):
                total = total + given[i, at : at + rows].astype(F32)
            out[j, k * rows : (k + 1) * rows] = total.astype(BF16)
    start = members * blocks * rows
    piece = given[0, start:].astype(F32)
    for i in range(1, given.shape[0]):
        piece = piece + given[i, start:].astype(F32)
    for j in range(members):
        out[j, blocks * rows :] = piece.astype(BF16)


def far_sum(given, own_term, input_grad, pieces, *, factor):
    rows = own_term.shape[0]
    total = own_term[...]
    piece = given[0, rows:].astype(F32)
    for j in range(given.shape[0]):
        total = total + given[j, :rows].astype(F32)
        if j > 0:
            piece = piece + given[j, rows:].astype(F32)
    input_grad[...] = total.astype(BF16)
    piece = (piece * factor).astype(BF16)
    for i in range(pieces.shape[0]):
        pieces[i] = piece


def lay(given, grad_self, grad_neigh):
    _, high, wide = given.shape
    lanes = grad_self.shape[1] // wide
    half = given.shape[0] // 2
    for i in range(half):
        g, q = divmod(i, lanes)
        grad_self[g * high : (g + 1) * high, q * wide : (q + 1) * wide] = given[i].astype(F32)
        grad_neigh[g * high : (g + 1) * high, q * wide : (q + 1) * wide] = given[half + i].astype(F32)


def run(kernel, outs, scalars, arrays, scratch=(), name=None):
    vmem = pl.BlockSpec(memory_space=pltpu.VMEM)
    smem = pl.BlockSpec(memory_space=pltpu.SMEM)
    return pl.pallas_call(
        kernel,
        out_shape=tuple(jax.ShapeDtypeStruct(shape, kind) for shape, kind in outs),
        in_specs=[smem] * len(scalars) + [vmem] * len(arrays),
        out_specs=(vmem,) * len(outs),
        scratch_shapes=[pltpu.VMEM(shape, kind) for shape, kind in scratch],
        compiler_params=pltpu.CompilerParams(vmem_limit_bytes=32 * 1024 * 1024),
        name=name,
    )(*scalars, *arrays)


def spread(array, axes):
    parts = count(axes)
    return lax.all_to_all(jnp.broadcast_to(array[None], (parts, *array.shape)), axes, 0, 0)


def body(features, cotangent, w_self, w_neigh, tile_cols, tile_edges, degrees):
    rows, size = features.shape
    total = w_self.shape[0]
    reps = total // rows
    blocks, near_count, mid_count, far_count = math.prod(LOOP), count(NEAR), count(MID), count(FAR)
    degrees = degrees.reshape(1, size)
    here = jnp.stack([lax.axis_index("rep").astype(jnp.int32), lax.axis_index("c").astype(jnp.int32)])
    swap = [(0, 1), (1, 0)]
    panel = (rows, size)

    near = spread(spread(features, MID + FAR), NEAR).reshape(blocks // 2, rows, size)
    far = lax.ppermute(near, "c", swap)
    sent, neighbours = run(
        combine,
        [((reps, 2, rows, size), BF16), (panel, BF16)],
        [tile_cols, here],
        [features, cotangent, degrees, tile_edges, near, far, w_self, w_neigh],
        name="combine",
    )
    parts = lax.all_to_all(sent, "rep", 0, 0)

    pieces = rows * (total // size) // near_count
    filled = mid_count * far_count * rows
    halves = ((near_count, filled + 2 * pieces, size), BF16)
    layer_out, own_term, mine, theirs = run(
        contribute,
        [(panel, BF16), (panel, F32), halves, halves],
        [tile_cols, here],
        [parts, features, neighbours, degrees, tile_edges, w_self, w_neigh],
        [((tile_edges.shape[1], rows, size), F32)],
        name="contribute",
    )
    given = lax.ppermute(theirs, "c", swap)
    sums = [((near_count, filled + pieces, size), BF16)]
    (sums,) = run(functools.partial(pair_sum, rows=rows), sums, [], [mine, given], name="pair_sum")
    add = functools.partial(stage_sum, rows=rows)
    given = lax.all_to_all(sums, NEAR, 0, 0)
    sums = [((mid_count, far_count * rows + pieces, size), BF16)]
    (sums,) = run(add, sums, [], [given], name="near_sum")
    given = lax.all_to_all(sums, MID, 0, 0)
    sums = [((far_count, rows + pieces, size), BF16)]
    (sums,) = run(add, sums, [], [given], name="mid_sum")
    given = lax.all_to_all(sums, FAR, 0, 0)

    input_grad, out = run(
        functools.partial(far_sum, factor=1.0 / math.sqrt(blocks * size)),
        [(panel, BF16), ((2 * near_count, pieces, size), BF16)],
        [],
        [given, own_term],
        name="far_sum",
    )
    given = lax.all_to_all(out, ("c", *NEAR), 0, 0)
    grad = ((rows, total), F32)
    grad_self, grad_neigh = run(lay, [grad, grad], [], [given], name="lay")
    return layer_out, input_grad, grad_self, grad_neigh


def solution(mesh):
    fine = Mesh(mesh.devices.reshape(*LOOP, mesh.shape["rep"]), (*AXES, "rep"))
    in_specs = (
        P("rep", AXES),
        P("rep", AXES),
        P(),
        P(),
        P(AXES, None),
        P(AXES, None, None, None),
        P(AXES),
    )
    out_specs = (P("rep", AXES), P("rep", AXES), P("rep", None), P("rep", None))
    return jax.shard_map(body, mesh=fine, in_specs=in_specs, out_specs=out_specs, check_vma=False)
```

```python
import functools
import math

import jax
import jax.numpy as jnp
from jax import lax
from jax.experimental import pallas as pl
from jax.experimental.pallas import tpu as pltpu
from jax.sharding import Mesh, PartitionSpec as P

F32, BF16 = jnp.float32, jnp.bfloat16
AXES = ("zh", "zm", "zl", "yh", "yl", "c")
LOOP = (4, 2, 2, 2, 2, 2)
NEAR, MID, FAR = ("zl", "yl"), ("zm", "yh"), ("zh",)


def count(axes):
    return math.prod(LOOP[AXES.index(axis)] for axis in axes)


def place(col):
    digit = {}
    for axis, extent in zip(reversed(AXES), reversed(LOOP)):
        digit[axis] = lax.rem(col, extent)
        col = lax.div(col, extent)
    near = far = jnp.int32(0)
    for axis in NEAR:
        near = near * LOOP[AXES.index(axis)] + digit[axis]
    for axis in MID + FAR:
        far = far * LOOP[AXES.index(axis)] + digit[axis]
    return digit["c"], near, far


def split(value):
    high = value.astype(BF16)
    return jnp.concatenate([high, (value - high.astype(F32)).astype(BF16)], 0)


def join(pair):
    half = pair.shape[0] // 2
    return pair[:half].astype(F32) + pair[half:].astype(F32)


def combine(cols, here, features, cot, degrees, tiles, w_self, w_neigh, *refs):
    *panels, out, neighbours = refs
    slots, rows, members = tiles.shape[1], features.shape[0], len(panels) // 2
    total = jnp.zeros(features.shape, F32)
    for k in range(slots):
        core, i, j = place(cols[0, k])
        source = jnp.bitwise_xor(i, here[2]) + jnp.where(core == here[1], 0, members)
        block = panels[0][j]
        for n in range(1, 2 * members):
            block = jnp.where(source == n, panels[n][j], block)
        total = total + lax.dot_general(
            block,
            tiles[0, k].astype(F32).astype(BF16),
            (((1,), (1,)), ((), ())),
            preferred_element_type=F32,
        )
    mean = (total / jnp.maximum(degrees[...].astype(F32), 1.0)).astype(BF16)
    neighbours[...] = mean
    own = pl.ds(pl.multiple_of(here[0] * rows, rows), rows)
    turned = (((0,), (0,)), ((), ()))
    forward = lax.dot_general(w_self[own, :], features[...], turned, preferred_element_type=F32)
    forward = forward + lax.dot_general(w_neigh[own, :], mean, turned, preferred_element_type=F32)
    for r in range(out.shape[0]):
        out[r, 0] = forward[r * rows : (r + 1) * rows].astype(BF16)
        out[r, 1] = cot[...]


def contribute(
    cols, here, parts, features, neighbours, degrees, tiles, w_self, w_neigh, layer_out, own_term, mine, theirs, held
):
    slots, rows, size = tiles.shape[1], features.shape[0], w_self.shape[0]
    members, filled = mine.shape[0], count(MID + FAR) * rows
    empty = jnp.zeros((rows, mine.shape[2]), BF16)

    def clear(i, _):
        for j in range(0, filled, rows):
            mine[i, j : j + rows] = empty
            theirs[i, j : j + rows] = empty
        return 0

    lax.fori_loop(0, members, clear, 0)
    forward = parts[0, 0].astype(F32)
    for r in range(1, parts.shape[0]):
        forward = forward + parts[r, 0].astype(F32)
    layer_out[...] = forward.astype(BF16)
    cot = parts[:, 1].reshape(size, parts.shape[3])
    own = pl.ds(pl.multiple_of(here[0] * rows, rows), rows)
    own_term[...] = jnp.dot(w_self[own, :], cot, preferred_element_type=F32)
    scaled = jnp.dot(w_neigh[own, :], cot, preferred_element_type=F32)
    both = split(scaled / jnp.maximum(degrees[...].astype(F32), 1.0))
    for k in range(slots):
        part = jnp.dot(both, tiles[0, k].astype(F32).astype(BF16), preferred_element_type=F32)
        held[k] = part[:rows] + part[rows:]
    first = []
    for k in range(slots):
        at = jnp.int32(k)
        for j in range(k - 1, -1, -1):
            at = jnp.where(cols[0, j] == cols[0, k], jnp.int32(j), at)
        first.append(at)
    for k in range(1, slots):

        @pl.when(first[k] != k)
        def _():
            held[first[k]] = held[first[k]] + held[k]

    for k in range(slots):
        core, i, j = place(cols[0, k])
        span = pl.ds(pl.multiple_of(j * rows, rows), rows)

        @pl.when((first[k] == k) & (core == here[1]))
        def _():
            mine[i, span, :] = held[k].astype(BF16)

        @pl.when((first[k] == k) & (core != here[1]))
        def _():
            theirs[i, span, :] = held[k].astype(BF16)

    wide = mine.shape[2]
    lanes = size // wide
    high = rows * lanes // members
    pair = jnp.concatenate([features[...], neighbours[...]], 0)
    for q in range(lanes):
        term = lax.dot_general(
            pair, cot[q * wide : (q + 1) * wide], (((1,), (1,)), ((), ())), preferred_element_type=F32
        )
        ours = jnp.where(here[1] == 0, term[:rows], term[rows:])
        other = jnp.where(here[1] == 0, term[rows:], term[:rows])
        for g in range(members // lanes):
            mine[g * lanes + q, filled:] = split(ours[g * high : (g + 1) * high])
            theirs[g * lanes + q, filled:] = split(other[g * high : (g + 1) * high])


def pair_sum(here, mine, given, *outs, rows):
    filled = count(MID + FAR) * rows
    for k, out in enumerate(outs):
        i = jnp.bitwise_xor(here[2], k)

        def step(j, _, i=i, out=out):
            span = pl.ds(pl.multiple_of(j * rows, rows), rows)
            out[span, :] = (mine[i, span, :].astype(F32) + given[i, span, :].astype(F32)).astype(BF16)
            return 0

        lax.fori_loop(0, filled // rows, step, 0)
        out[filled:] = (join(mine[i, filled:]) + join(given[i, filled:])).astype(BF16)


def stage_sum(*refs, rows):
    *given, out = refs
    if len(given[0].shape) == 3:
        given = [given[0].at[i] for i in range(given[0].shape[0])]
    members = out.shape[0]
    blocks = (given[0].shape[0] - out.shape[1]) // ((members - 1) * rows) if members > 1 else 1

    def added(at, high):
        total = given[0][at : at + high].astype(F32)
        for ref in given[1:]:
            total = total + ref[at : at + high].astype(F32)
        return total.astype(BF16)

    for j in range(members):
        for k in range(blocks):
            out[j, k * rows : (k + 1) * rows] = added((j * blocks + k) * rows, rows)
    start = members * blocks * rows
    piece = added(start, given[0].shape[0] - start)
    for j in range(members):
        out[j, blocks * rows :] = piece


def far_sum(given, own_term, input_grad, pieces, *, factor):
    rows = own_term.shape[0]
    total = own_term[...]
    piece = given[0, rows:].astype(F32)
    for j in range(given.shape[0]):
        total = total + given[j, :rows].astype(F32)
        if j > 0:
            piece = piece + given[j, rows:].astype(F32)
    input_grad[...] = total.astype(BF16)
    piece = (piece * factor).astype(BF16)
    for i in range(pieces.shape[0]):
        pieces[i] = piece


def lay(given, grad_self, grad_neigh):
    _, high, wide = given.shape
    lanes = grad_self.shape[1] // wide
    half = given.shape[0] // 2
    for i in range(half):
        g, q = divmod(i, lanes)
        grad_self[g * high : (g + 1) * high, q * wide : (q + 1) * wide] = given[i].astype(F32)
        grad_neigh[g * high : (g + 1) * high, q * wide : (q + 1) * wide] = given[half + i].astype(F32)


def run(kernel, outs, scalars, arrays, scratch=(), name=None):
    vmem = pl.BlockSpec(memory_space=pltpu.VMEM)
    smem = pl.BlockSpec(memory_space=pltpu.SMEM)
    return pl.pallas_call(
        kernel,
        out_shape=tuple(jax.ShapeDtypeStruct(shape, kind) for shape, kind in outs),
        in_specs=[smem] * len(scalars) + [vmem] * len(arrays),
        out_specs=(vmem,) * len(outs),
        scratch_shapes=[pltpu.VMEM(shape, kind) for shape, kind in scratch],
        compiler_params=pltpu.CompilerParams(vmem_limit_bytes=32 * 1024 * 1024),
        name=name,
    )(*scalars, *arrays)


def spread(array, axes):
    parts = count(axes)
    return lax.all_to_all(jnp.broadcast_to(array[None], (parts, *array.shape)), axes, 0, 0)


def body(features, cotangent, w_self, w_neigh, tile_cols, tile_edges, degrees):
    rows, size = features.shape
    total = w_self.shape[0]
    reps = total // rows
    blocks, near_count, mid_count, far_count = math.prod(LOOP), count(NEAR), count(MID), count(FAR)
    degrees = degrees.reshape(1, size)
    here = jnp.stack([lax.axis_index(axes).astype(jnp.int32) for axes in ("rep", "c", NEAR)])
    swap = [(0, 1), (1, 0)]
    panel = (rows, size)


    def flip(array, k):
        return lax.ppermute(array, NEAR, [(i, i ^ k) for i in range(near_count)])

    panels = spread(features, MID + FAR)
    near = [panels] + [flip(panels, k) for k in range(1, near_count)]
    far = [lax.ppermute(array, "c", swap) for array in near]
    sent, neighbours = run(
        combine,
        [((reps, 2, rows, size), BF16), (panel, BF16)],
        [tile_cols, here],
        [features, cotangent, degrees, tile_edges, w_self, w_neigh, *near, *far],
        name="combine",
    )
    parts = lax.all_to_all(sent, "rep", 0, 0)

    pieces = rows * (total // size) // near_count
    filled = mid_count * far_count * rows
    halves = ((near_count, filled + 2 * pieces, size), BF16)
    layer_out, own_term, mine, theirs = run(
        contribute,
        [(panel, BF16), (panel, F32), halves, halves],
        [tile_cols, here],
        [parts, features, neighbours, degrees, tile_edges, w_self, w_neigh],
        [((tile_edges.shape[1], rows, size), F32)],
        name="contribute",
    )
    given = lax.ppermute(theirs, "c", swap)
    sums = [((filled + pieces, size), BF16)] * near_count
    sums = run(functools.partial(pair_sum, rows=rows), sums, [here], [mine, given], name="pair_sum")
    add = functools.partial(stage_sum, rows=rows)
    given = [sums[0]] + [flip(sums[k], k) for k in range(1, near_count)]
    sums = [((mid_count, far_count * rows + pieces, size), BF16)]
    (sums,) = run(add, sums, [], given, name="near_sum")
    given = lax.all_to_all(sums, MID, 0, 0)
    sums = [((far_count, rows + pieces, size), BF16)]
    (sums,) = run(add, sums, [], [given], name="mid_sum")
    given = lax.all_to_all(sums, FAR, 0, 0)

    input_grad, out = run(
        functools.partial(far_sum, factor=1.0 / math.sqrt(blocks * size)),
        [(panel, BF16), ((2 * near_count, pieces, size), BF16)],
        [],
        [given, own_term],
        name="far_sum",
    )
    given = lax.all_to_all(out, ("c", *NEAR), 0, 0)
    grad = ((rows, total), F32)
    grad_self, grad_neigh = run(lay, [grad, grad], [], [given], name="lay")
    return layer_out, input_grad, grad_self, grad_neigh


def solution(mesh):
    fine = Mesh(mesh.devices.reshape(*LOOP, mesh.shape["rep"]), (*AXES, "rep"))
    in_specs = (
        P("rep", AXES),
        P("rep", AXES),
        P(),
        P(),
        P(AXES, None),
        P(AXES, None, None, None),
        P(AXES),
    )
    out_specs = (P("rep", AXES), P("rep", AXES), P("rep", None), P("rep", None))
    return jax.shard_map(body, mesh=fine, in_specs=in_specs, out_specs=out_specs, check_vma=False)
```

```python
import functools
import math

import jax
import jax.numpy as jnp
from jax import lax
from jax.experimental import pallas as pl
from jax.experimental.pallas import tpu as pltpu
from jax.sharding import Mesh, PartitionSpec as P

F32, BF16 = jnp.float32, jnp.bfloat16
AXES = ("zh", "zm", "zl", "yh", "yl", "c")
LOOP = (4, 2, 2, 2, 2, 2)
NEAR, MID, FAR = ("yl", "zl"), ("zm", "yh"), ("zh",)


def count(axes):
    return math.prod(LOOP[AXES.index(axis)] for axis in axes)


def place(col):
    digit = {}
    for axis, extent in zip(reversed(AXES), reversed(LOOP)):
        digit[axis] = lax.rem(col, extent)
        col = lax.div(col, extent)
    near = far = jnp.int32(0)
    for axis in NEAR:
        near = near * LOOP[AXES.index(axis)] + digit[axis]
    for axis in MID + FAR:
        far = far * LOOP[AXES.index(axis)] + digit[axis]
    return digit["c"], near, far


def split(value):
    high = value.astype(BF16)
    return jnp.concatenate([high, (value - high.astype(F32)).astype(BF16)], 0)


def join(pair):
    half = pair.shape[0] // 2
    return pair[:half].astype(F32) + pair[half:].astype(F32)


def widen(tiles, out):
    wide = tiles.shape[3]
    for k in range(tiles.shape[1]):
        out[:, k * wide : (k + 1) * wide] = tiles[0, k].astype(F32).astype(BF16)


def combine(cols, here, features, cot, degrees, tiles, near, far, w_self, w_neigh, out, neighbours, chosen):
    rows, wide = features.shape
    for k in range(cols.shape[1]):
        core, i, j = place(cols[0, k])
        at = i * count(MID + FAR) + j
        chosen[:, k * wide : (k + 1) * wide] = jnp.where(core == here[1], near[at], far[at])
    total = lax.dot_general(chosen[...], tiles[...], (((1,), (1,)), ((), ())), preferred_element_type=F32)
    mean = (total / jnp.maximum(degrees[...].astype(F32), 1.0)).astype(BF16)
    neighbours[...] = mean
    own = pl.ds(pl.multiple_of(here[0] * rows, rows), rows)
    flip = (((0,), (0,)), ((), ()))
    forward = lax.dot_general(w_self[own, :], features[...], flip, preferred_element_type=F32)
    forward = forward + lax.dot_general(w_neigh[own, :], mean, flip, preferred_element_type=F32)
    for r in range(out.shape[0]):
        out[r, 0] = forward[r * rows : (r + 1) * rows].astype(BF16)
        out[r, 1] = cot[...]


def contribute(
    cols, here, parts, features, neighbours, degrees, tiles, w_self, w_neigh, layer_out, own_term, mine, theirs, held
):
    slots, rows, size = cols.shape[1], features.shape[0], w_self.shape[0]
    members, filled = mine.shape[0], count(MID + FAR) * rows
    empty = jnp.zeros((rows, mine.shape[2]), BF16)

    def clear(i, _):
        for j in range(0, filled, rows):
            mine[i, j : j + rows] = empty
            theirs[i, j : j + rows] = empty
        return 0

    lax.fori_loop(0, members, clear, 0)
    forward = parts[0, 0].astype(F32)
    for r in range(1, parts.shape[0]):
        forward = forward + parts[r, 0].astype(F32)
    layer_out[...] = forward.astype(BF16)
    cot = parts[:, 1].reshape(size, parts.shape[3])
    own = pl.ds(pl.multiple_of(here[0] * rows, rows), rows)
    own_term[...] = jnp.dot(w_self[own, :], cot, preferred_element_type=F32)
    scaled = jnp.dot(w_neigh[own, :], cot, preferred_element_type=F32)
    both = split(scaled / jnp.maximum(degrees[...].astype(F32), 1.0))
    part = jnp.dot(both, tiles[...], preferred_element_type=F32)
    wide = mine.shape[2]
    for k in range(slots):
        held[k] = part[:rows, k * wide : (k + 1) * wide] + part[rows:, k * wide : (k + 1) * wide]
    first = []
    for k in range(slots):
        at = jnp.int32(k)
        for j in range(k - 1, -1, -1):
            at = jnp.where(cols[0, j] == cols[0, k], jnp.int32(j), at)
        first.append(at)
    for k in range(1, slots):

        @pl.when(first[k] != k)
        def _():
            held[first[k]] = held[first[k]] + held[k]

    for k in range(slots):
        core, i, j = place(cols[0, k])
        span = pl.ds(pl.multiple_of(j * rows, rows), rows)

        @pl.when((first[k] == k) & (core == here[1]))
        def _():
            mine[i, span, :] = held[k].astype(BF16)

        @pl.when((first[k] == k) & (core != here[1]))
        def _():
            theirs[i, span, :] = held[k].astype(BF16)

    lanes = size // wide
    high = rows * lanes // members
    pair = jnp.concatenate([features[...], neighbours[...]], 0)
    for q in range(lanes):
        term = lax.dot_general(
            pair, cot[q * wide : (q + 1) * wide], (((1,), (1,)), ((), ())), preferred_element_type=F32
        )
        ours = jnp.where(here[1] == 0, term[:rows], term[rows:])
        other = jnp.where(here[1] == 0, term[rows:], term[:rows])
        for g in range(members // lanes):
            mine[g * lanes + q, filled:] = split(ours[g * high : (g + 1) * high])
            theirs[g * lanes + q, filled:] = split(other[g * high : (g + 1) * high])


def pair_sum(mine, given, out, *, rows):
    filled = count(MID + FAR) * rows

    def step(i, _):
        for j in range(0, filled, rows):
            block = mine[i, j : j + rows].astype(F32) + given[i, j : j + rows].astype(F32)
            out[i, j : j + rows] = block.astype(BF16)
        out[i, filled:] = (join(mine[i, filled:]) + join(given[i, filled:])).astype(BF16)
        return 0

    lax.fori_loop(0, out.shape[0], step, 0)


def stage_sum(given, out, *, rows):
    members = out.shape[0]
    blocks = (given.shape[1] - out.shape[1]) // ((members - 1) * rows) if members > 1 else 1
    for j in range(members):
        for k in range(blocks):
            at = (j * blocks + k) * rows
            total = given[0, at : at + rows].astype(F32)
            for i in range(1, given.shape[0]):
                total = total + given[i, at : at + rows].astype(F32)
            out[j, k * rows : (k + 1) * rows] = total.astype(BF16)
    start = members * blocks * rows
    piece = given[0, start:].astype(F32)
    for i in range(1, given.shape[0]):
        piece = piece + given[i, start:].astype(F32)
    for j in range(members):
        out[j, blocks * rows :] = piece.astype(BF16)


def far_sum(given, own_term, input_grad, pieces, *, factor):
    rows = own_term.shape[0]
    total = own_term[...]
    piece = given[0, rows:].astype(F32)
    for j in range(given.shape[0]):
        total = total + given[j, :rows].astype(F32)
        if j > 0:
            piece = piece + given[j, rows:].astype(F32)
    input_grad[...] = total.astype(BF16)
    piece = (piece * factor).astype(BF16)
    for i in range(pieces.shape[0]):
        pieces[i] = piece


def lay(given, grad_self, grad_neigh):
    _, high, wide = given.shape
    lanes = grad_self.shape[1] // wide
    half = given.shape[0] // 2
    for i in range(half):
        g, q = divmod(i, lanes)
        grad_self[g * high : (g + 1) * high, q * wide : (q + 1) * wide] = given[i].astype(F32)
        grad_neigh[g * high : (g + 1) * high, q * wide : (q + 1) * wide] = given[half + i].astype(F32)


def run(kernel, outs, scalars, arrays, scratch=(), name=None):
    vmem = pl.BlockSpec(memory_space=pltpu.VMEM)
    smem = pl.BlockSpec(memory_space=pltpu.SMEM)
    return pl.pallas_call(
        kernel,
        out_shape=tuple(jax.ShapeDtypeStruct(shape, kind) for shape, kind in outs),
        in_specs=[smem] * len(scalars) + [vmem] * len(arrays),
        out_specs=(vmem,) * len(outs),
        scratch_shapes=[pltpu.VMEM(shape, kind) for shape, kind in scratch],
        compiler_params=pltpu.CompilerParams(vmem_limit_bytes=32 * 1024 * 1024),
        name=name,
    )(*scalars, *arrays)


def spread(array, axes):
    parts = count(axes)
    return lax.all_to_all(jnp.broadcast_to(array[None], (parts, *array.shape)), axes, 0, 0)


def body(features, cotangent, w_self, w_neigh, tile_cols, tile_edges, degrees):
    rows, size = features.shape
    total = w_self.shape[0]
    reps = total // rows
    blocks, near_count, mid_count, far_count = math.prod(LOOP), count(NEAR), count(MID), count(FAR)
    degrees = degrees.reshape(1, size)
    here = jnp.stack([lax.axis_index("rep").astype(jnp.int32), lax.axis_index("c").astype(jnp.int32)])
    swap = [(0, 1), (1, 0)]
    panel = (rows, size)

    slots = tile_cols.shape[1]
    (tiles,) = run(widen, [((size, slots * size), BF16)], [], [tile_edges], name="widen")
    near = spread(spread(features, MID + FAR), NEAR).reshape(blocks // 2, rows, size)
    far = lax.ppermute(near, "c", swap)
    sent, neighbours = run(
        combine,
        [((reps, 2, rows, size), BF16), (panel, BF16)],
        [tile_cols, here],
        [features, cotangent, degrees, tiles, near, far, w_self, w_neigh],
        [((rows, slots * size), BF16)],
        name="combine",
    )
    parts = lax.all_to_all(sent, "rep", 0, 0)

    pieces = rows * (total // size) // near_count
    filled = mid_count * far_count * rows
    halves = ((near_count, filled + 2 * pieces, size), BF16)
    layer_out, own_term, mine, theirs = run(
        contribute,
        [(panel, BF16), (panel, F32), halves, halves],
        [tile_cols, here],
        [parts, features, neighbours, degrees, tiles, w_self, w_neigh],
        [((slots, rows, size), F32)],
        name="contribute",
    )
    given = lax.ppermute(theirs, "c", swap)
    sums = [((near_count, filled + pieces, size), BF16)]
    (sums,) = run(functools.partial(pair_sum, rows=rows), sums, [], [mine, given], name="pair_sum")
    add = functools.partial(stage_sum, rows=rows)
    given = lax.all_to_all(sums, NEAR, 0, 0)
    sums = [((mid_count, far_count * rows + pieces, size), BF16)]
    (sums,) = run(add, sums, [], [given], name="near_sum")
    given = lax.all_to_all(sums, MID, 0, 0)
    sums = [((far_count, rows + pieces, size), BF16)]
    (sums,) = run(add, sums, [], [given], name="mid_sum")
    given = lax.all_to_all(sums, FAR, 0, 0)

    input_grad, out = run(
        functools.partial(far_sum, factor=1.0 / math.sqrt(blocks * size)),
        [(panel, BF16), ((2 * near_count, pieces, size), BF16)],
        [],
        [given, own_term],
        name="far_sum",
    )
    given = lax.all_to_all(out, ("c", *NEAR), 0, 0)
    grad = ((rows, total), F32)
    grad_self, grad_neigh = run(lay, [grad, grad], [], [given], name="lay")
    return layer_out, input_grad, grad_self, grad_neigh


def solution(mesh):
    fine = Mesh(mesh.devices.reshape(*LOOP, mesh.shape["rep"]), (*AXES, "rep"))
    in_specs = (
        P("rep", AXES),
        P("rep", AXES),
        P(),
        P(),
        P(AXES, None),
        P(AXES, None, None, None),
        P(AXES),
    )
    out_specs = (P("rep", AXES), P("rep", AXES), P("rep", None), P("rep", None))
    return jax.shard_map(body, mesh=fine, in_specs=in_specs, out_specs=out_specs, check_vma=False)
```

```python
import functools
import math

import jax
import jax.numpy as jnp
from jax import lax
from jax.experimental import pallas as pl
from jax.experimental.pallas import tpu as pltpu
from jax.sharding import Mesh, PartitionSpec as P

F32, BF16 = jnp.float32, jnp.bfloat16
AXES = ("zh", "zm", "zl", "yh", "yl", "c")
LOOP = (4, 2, 2, 2, 2, 2)
NEAR, MID, FAR = ("yl", "zl"), ("zm", "yh"), ("zh",)


def count(axes):
    return math.prod(LOOP[AXES.index(axis)] for axis in axes)


def place(col):
    digit = {}
    for axis, extent in zip(reversed(AXES), reversed(LOOP)):
        digit[axis] = lax.rem(col, extent)
        col = lax.div(col, extent)
    near = far = jnp.int32(0)
    for axis in NEAR:
        near = near * LOOP[AXES.index(axis)] + digit[axis]
    for axis in MID + FAR:
        far = far * LOOP[AXES.index(axis)] + digit[axis]
    return digit["c"], near, far


def split(value):
    high = value.astype(BF16)
    return jnp.concatenate([high, (value - high.astype(F32)).astype(BF16)], 0)


def join(pair):
    half = pair.shape[0] // 2
    return pair[:half].astype(F32) + pair[half:].astype(F32)


def widen(tiles, out):
    wide = tiles.shape[3]
    for k in range(tiles.shape[1]):
        out[:, k * wide : (k + 1) * wide] = tiles[0, k].astype(F32).astype(BF16)


def combine(cols, here, features, cot, degrees, tiles, near, far, w_self, w_neigh, out, neighbours, chosen):
    rows, wide = features.shape
    for k in range(cols.shape[1]):
        core, i, j = place(cols[0, k])
        at = i * count(MID + FAR) + j
        chosen[:, k * wide : (k + 1) * wide] = jnp.where(core == here[1], near[at], far[at])
    total = lax.dot_general(chosen[...], tiles[...], (((1,), (1,)), ((), ())), preferred_element_type=F32)
    mean = (total / jnp.maximum(degrees[...].astype(F32), 1.0)).astype(BF16)
    neighbours[...] = mean
    own = pl.ds(pl.multiple_of(here[0] * rows, rows), rows)
    flip = (((0,), (0,)), ((), ()))
    forward = lax.dot_general(w_self[own, :], features[...], flip, preferred_element_type=F32)
    forward = forward + lax.dot_general(w_neigh[own, :], mean, flip, preferred_element_type=F32)
    for r in range(out.shape[0]):
        out[r, 0] = forward[r * rows : (r + 1) * rows].astype(BF16)
        out[r, 1] = cot[...]


def contribute(
    cols, here, parts, features, neighbours, degrees, tiles, w_self, w_neigh, own_term, mine, theirs, held
):
    slots, rows, size = cols.shape[1], features.shape[0], w_self.shape[0]
    members, filled = mine.shape[0], count(MID + FAR) * rows
    empty = jnp.zeros((rows, mine.shape[2]), BF16)

    def clear(i, _):
        for j in range(0, filled, rows):
            mine[i, j : j + rows] = empty
            theirs[i, j : j + rows] = empty
        return 0

    lax.fori_loop(0, members, clear, 0)
    cot = parts[:, 1].reshape(size, parts.shape[3])
    own = pl.ds(pl.multiple_of(here[0] * rows, rows), rows)
    own_term[...] = jnp.dot(w_self[own, :], cot, preferred_element_type=F32)
    scaled = jnp.dot(w_neigh[own, :], cot, preferred_element_type=F32)
    both = split(scaled / jnp.maximum(degrees[...].astype(F32), 1.0))
    part = jnp.dot(both, tiles[...], preferred_element_type=F32)
    wide = mine.shape[2]
    for k in range(slots):
        held[k] = part[:rows, k * wide : (k + 1) * wide] + part[rows:, k * wide : (k + 1) * wide]
    first = []
    for k in range(slots):
        at = jnp.int32(k)
        for j in range(k - 1, -1, -1):
            at = jnp.where(cols[0, j] == cols[0, k], jnp.int32(j), at)
        first.append(at)
    for k in range(1, slots):

        @pl.when(first[k] != k)
        def _():
            held[first[k]] = held[first[k]] + held[k]

    for k in range(slots):
        core, i, j = place(cols[0, k])
        span = pl.ds(pl.multiple_of(j * rows, rows), rows)

        @pl.when((first[k] == k) & (core == here[1]))
        def _():
            mine[i, span, :] = held[k].astype(BF16)

        @pl.when((first[k] == k) & (core != here[1]))
        def _():
            theirs[i, span, :] = held[k].astype(BF16)

    lanes = size // wide
    high = rows * lanes // members
    pair = jnp.concatenate([features[...], neighbours[...]], 0)
    for q in range(lanes):
        term = lax.dot_general(
            pair, cot[q * wide : (q + 1) * wide], (((1,), (1,)), ((), ())), preferred_element_type=F32
        )
        ours = jnp.where(here[1] == 0, term[:rows], term[rows:])
        other = jnp.where(here[1] == 0, term[rows:], term[:rows])
        for g in range(members // lanes):
            mine[g * lanes + q, filled:] = split(ours[g * high : (g + 1) * high])
            theirs[g * lanes + q, filled:] = split(other[g * high : (g + 1) * high])


def pair_sum(mine, given, out, *, rows):
    filled = count(MID + FAR) * rows

    def step(i, _):
        for j in range(0, filled, rows):
            block = mine[i, j : j + rows].astype(F32) + given[i, j : j + rows].astype(F32)
            out[i, j : j + rows] = block.astype(BF16)
        out[i, filled:] = (join(mine[i, filled:]) + join(given[i, filled:])).astype(BF16)
        return 0

    lax.fori_loop(0, out.shape[0], step, 0)


def stage_sum(given, out, *, rows):
    members = out.shape[0]
    blocks = (given.shape[1] - out.shape[1]) // ((members - 1) * rows) if members > 1 else 1
    for j in range(members):
        for k in range(blocks):
            at = (j * blocks + k) * rows
            total = given[0, at : at + rows].astype(F32)
            for i in range(1, given.shape[0]):
                total = total + given[i, at : at + rows].astype(F32)
            out[j, k * rows : (k + 1) * rows] = total.astype(BF16)
    start = members * blocks * rows
    piece = given[0, start:].astype(F32)
    for i in range(1, given.shape[0]):
        piece = piece + given[i, start:].astype(F32)
    for j in range(members):
        out[j, blocks * rows :] = piece.astype(BF16)


def far_sum(given, pieces, *, rows, factor):
    piece = given[0, rows:].astype(F32)
    for j in range(1, given.shape[0]):
        piece = piece + given[j, rows:].astype(F32)
    piece = (piece * factor).astype(BF16)
    for i in range(pieces.shape[0]):
        pieces[i] = piece


def close(given, own_term, parts, input_grad, layer_out):
    total = own_term[...]
    for j in range(given.shape[0]):
        total = total + given[j, : total.shape[0]].astype(F32)
    input_grad[...] = total.astype(BF16)
    forward = parts[0, 0].astype(F32)
    for r in range(1, parts.shape[0]):
        forward = forward + parts[r, 0].astype(F32)
    layer_out[...] = forward.astype(BF16)


def lay(given, grad_self, grad_neigh):
    _, high, wide = given.shape
    lanes = grad_self.shape[1] // wide
    half = given.shape[0] // 2
    for i in range(half):
        g, q = divmod(i, lanes)
        grad_self[g * high : (g + 1) * high, q * wide : (q + 1) * wide] = given[i].astype(F32)
        grad_neigh[g * high : (g + 1) * high, q * wide : (q + 1) * wide] = given[half + i].astype(F32)


def run(kernel, outs, scalars, arrays, scratch=(), name=None):
    vmem = pl.BlockSpec(memory_space=pltpu.VMEM)
    smem = pl.BlockSpec(memory_space=pltpu.SMEM)
    return pl.pallas_call(
        kernel,
        out_shape=tuple(jax.ShapeDtypeStruct(shape, kind) for shape, kind in outs),
        in_specs=[smem] * len(scalars) + [vmem] * len(arrays),
        out_specs=(vmem,) * len(outs),
        scratch_shapes=[pltpu.VMEM(shape, kind) for shape, kind in scratch],
        compiler_params=pltpu.CompilerParams(vmem_limit_bytes=32 * 1024 * 1024),
        name=name,
    )(*scalars, *arrays)


def spread(array, axes):
    parts = count(axes)
    return lax.all_to_all(jnp.broadcast_to(array[None], (parts, *array.shape)), axes, 0, 0)


def body(features, cotangent, w_self, w_neigh, tile_cols, tile_edges, degrees):
    rows, size = features.shape
    total = w_self.shape[0]
    reps = total // rows
    blocks, near_count, mid_count, far_count = math.prod(LOOP), count(NEAR), count(MID), count(FAR)
    degrees = degrees.reshape(1, size)
    here = jnp.stack([lax.axis_index("rep").astype(jnp.int32), lax.axis_index("c").astype(jnp.int32)])
    swap = [(0, 1), (1, 0)]
    panel = (rows, size)

    slots = tile_cols.shape[1]
    (tiles,) = run(widen, [((size, slots * size), BF16)], [], [tile_edges], name="widen")
    near = spread(spread(features, MID + FAR), NEAR).reshape(blocks // 2, rows, size)
    far = lax.ppermute(near, "c", swap)
    sent, neighbours = run(
        combine,
        [((reps, 2, rows, size), BF16), (panel, BF16)],
        [tile_cols, here],
        [features, cotangent, degrees, tiles, near, far, w_self, w_neigh],
        [((rows, slots * size), BF16)],
        name="combine",
    )
    parts = lax.all_to_all(sent, "rep", 0, 0)

    pieces = rows * (total // size) // near_count
    filled = mid_count * far_count * rows
    halves = ((near_count, filled + 2 * pieces, size), BF16)
    own_term, mine, theirs = run(
        contribute,
        [(panel, F32), halves, halves],
        [tile_cols, here],
        [parts, features, neighbours, degrees, tiles, w_self, w_neigh],
        [((slots, rows, size), F32)],
        name="contribute",
    )
    given = lax.ppermute(theirs, "c", swap)
    sums = [((near_count, filled + pieces, size), BF16)]
    (sums,) = run(functools.partial(pair_sum, rows=rows), sums, [], [mine, given], name="pair_sum")
    add = functools.partial(stage_sum, rows=rows)
    given = lax.all_to_all(sums, NEAR, 0, 0)
    sums = [((mid_count, far_count * rows + pieces, size), BF16)]
    (sums,) = run(add, sums, [], [given], name="near_sum")
    given = lax.all_to_all(sums, MID, 0, 0)
    sums = [((far_count, rows + pieces, size), BF16)]
    (sums,) = run(add, sums, [], [given], name="mid_sum")
    given = lax.all_to_all(sums, FAR, 0, 0)

    (out,) = run(
        functools.partial(far_sum, rows=rows, factor=1.0 / math.sqrt(blocks * size)),
        [((2 * near_count, pieces, size), BF16)],
        [],
        [given],
        name="far_sum",
    )
    input_grad, layer_out = run(
        close, [(panel, BF16), (panel, BF16)], [], [given, own_term, parts], name="close"
    )
    given = lax.all_to_all(out, ("c", *NEAR), 0, 0)
    grad = ((rows, total), F32)
    grad_self, grad_neigh = run(lay, [grad, grad], [], [given], name="lay")
    return layer_out, input_grad, grad_self, grad_neigh


def solution(mesh):
    fine = Mesh(mesh.devices.reshape(*LOOP, mesh.shape["rep"]), (*AXES, "rep"))
    in_specs = (
        P("rep", AXES),
        P("rep", AXES),
        P(),
        P(),
        P(AXES, None),
        P(AXES, None, None, None),
        P(AXES),
    )
    out_specs = (P("rep", AXES), P("rep", AXES), P("rep", None), P("rep", None))
    return jax.shard_map(body, mesh=fine, in_specs=in_specs, out_specs=out_specs, check_vma=False)
```
